512 devices in a mesh: bank: 128 (over x, z_lo, y), det: 4 (over z_hi, core).
Axes of the slice: x: 4, y: 4, z: 16 (z_hi: 2, z_lo: 8; z = z_hi * 8 + z_lo), core: 2. Of those that a mesh axis runs over, the one named last changes fastest.
Arguments:
- strain: float32 [4, 256, 2, 256], P('det', 'bank'), may hold values from -4 to 4
- inverse_noise: float32 [4, 256, 256], P('det', 'bank'), may hold values from 0.4 to 4
- slides: int32 [4], P('det'), may hold values from 0 to 131071
- templates: float32 [512, 256, 2, 256], P(('bank', 'det')), may hold values from -6 to 6
- cutoffs: int32 [512], P(('bank', 'det')), may hold values from 16384 to 65536
Outputs:
- loudest: float32 [131072], P('bank')
- network: float32 [512, 131072], P(('bank', 'det'))
The draws below stay inside these ranges and needn't reach their ends.
All inputs are finite; a program needn't handle non-finite values.
Results may differ from the reference program's by a relative error of at most 0.0003.
Values sent between devices are 32-bit elements; how exact they have to be, the bound alone decides.
No kernel may reach another device: no remote copies, remote signals or barrier semaphores. Data moves between devices by JAX's collectives and lax.ppermute only.
A program may use at most 64 MiB of HBM per device.

```python
import math
import jax
import jax.numpy as jnp
from jax import lax

ROWS = 256
COLS = 256
DETS = 4
TEMPLATES = 512
BINS = 65536
SERIES = 131072


def touch_ends(values, rng, low, top_value):
    longest = values.shape.index(max(values.shape))
    spots = []
    for shift in (0, 1):
        where = [jax.random.randint(jax.random.fold_in(rng, axis), (), 0, length) for axis, length in enumerate(values.shape)]
        where[longest] = (where[longest] + shift) % values.shape[longest]
        spots.append(tuple(where))
    return values.at[spots[0]].set(low).at[spots[1]].set(top_value)


def block_scale(stream_key, dims, pieces, least, high):
    level = 1.0
    for dim, parts in pieces:
        steps = jax.random.uniform(jax.random.fold_in(jax.random.fold_in(stream_key, 6), dim), (parts,), jnp.float32, least / len(pieces), high / len(pieces))
        level = level * jnp.repeat(jnp.exp(steps), dims[dim] // parts).reshape((-1,) + (1,) * (len(dims) - 1 - dim))
    return level


def scatter_about(key, dims, spread, limit, cuts=(), kind=jnp.bfloat16):
    values = spread * jax.random.normal(key, dims, jnp.float32)
    if cuts:
        values = values * block_scale(key, dims, cuts, -0.22, 0.18)
    return jnp.clip(values, -limit, limit).astype(kind)


def setup_inputs(seed: int = 0) -> dict:
    key_of = jax.random.split(jax.random.key(seed), 6)
    strain = scatter_about(key_of[0], (DETS, ROWS, 2, COLS), 0.5, 4.0, ((0, 4), (1, 128)), jnp.float32)
    inverse_noise = jnp.clip(jnp.exp(math.log(4.0) - 2.3025851 * jax.random.uniform(key_of[1], (DETS, ROWS, COLS), jnp.float32) ** block_scale(key_of[1], (DETS, ROWS, COLS), ((0, 4), (1, 128)), -0.2, 0.2)), 0.4, 4.0)
    slides = touch_ends(jax.random.randint(key_of[2], (DETS,), 0, SERIES), jax.random.fold_in(key_of[2], 1), 0, SERIES - 1).astype(jnp.int32)
    templates = scatter_about(key_of[3], (TEMPLATES, ROWS, 2, COLS), 1.0, 6.0, ((0, 512),), jnp.float32)
    cutoffs = touch_ends(jax.random.randint(key_of[4], (TEMPLATES,), BINS // 4, BINS + 1), jax.random.fold_in(key_of[4], 1), BINS // 4, BINS).astype(jnp.int32)
    return dict(strain=strain, inverse_noise=inverse_noise, slides=slides, templates=templates, cutoffs=cutoffs)


def reference(strain, inverse_noise, slides, templates, cutoffs):
    series = 2 * ROWS * COLS
    bin_ids = jnp.arange(ROWS, dtype=jnp.int32)[:, None] * COLS + jnp.arange(COLS, dtype=jnp.int32)[None, :]
    data_re = strain[:, :, 0, :]
    data_im = strain[:, :, 1, :]

    def one_template(item):
        wave, cutoff = item
        bin_mask = (bin_ids < cutoff).astype(jnp.float32)
        weight = inverse_noise * bin_mask[None, :, :]
        wave_re = wave[None, :, 0, :]
        wave_im = wave[None, :, 1, :]
        prod_re = (data_re * wave_re + data_im * wave_im) * weight
        prod_im = (data_im * wave_re - data_re * wave_im) * weight
        energy = jnp.sum((wave_re * wave_re + wave_im * wave_im) * weight, axis=(1, 2))
        spectra = lax.complex(prod_re, prod_im).reshape(DETS, ROWS * COLS)
        spectra = jnp.concatenate([spectra, jnp.zeros_like(spectra)], axis=1)
        filtered = jnp.fft.ifft(spectra, axis=1) * series
        power = (jnp.real(filtered) ** 2 + jnp.imag(filtered) ** 2) / energy[:, None]
        network = jnp.roll(power[0], -slides[0])
        for index in range(1, DETS):
            network = network + jnp.roll(power[index], -slides[index])
        return network

    network = lax.map(one_template, (templates, cutoffs))
    return jnp.max(network, axis=0), network
```

```python
import jax
import jax.numpy as jnp
import ml_dtypes
import numpy as np
from jax import lax
from jax.experimental import pallas as pl
from jax.experimental.pallas import tpu as pltpu
from jax.sharding import Mesh, PartitionSpec as P

ROWS = 256
COLS = 256
SPAN = 512
SERIES = 131072
PLANE = ("x", "y")
PILE = ("zl", "zh")
CHIP = ("x", "y", "core")
STACK = ("zl", "zh", "core")


def split(values):
    high = values.astype(ml_dtypes.bfloat16)
    low = (values - high.astype(np.float64)).astype(ml_dtypes.bfloat16)
    return np.stack([high, low])


def plane_order():
    slot = np.arange(128)
    return slot // 32, slot // 8 % 4, slot % 8


def tables():
    x, y, zl = plane_order()
    first = []
    for parity in range(2):
        row = x * 64 + zl * 8 + y * 2 + parity
        angle = 2.0 * np.pi * (np.arange(256)[:, None] * row[None, :] % SPAN) / SPAN
        cos, sin = np.cos(angle), np.sin(angle)
        whole = []
        for chunk in range(2):
            part = slice(chunk * 128, chunk * 128 + 128)
            whole.append(np.block([[cos[part], -sin[part]], [sin[part], cos[part]]]))
        first.append(split(np.concatenate(whole)))
    first = np.stack(first)
    angle = 2.0 * np.pi * (np.arange(SPAN)[:, None] * np.arange(COLS)[None, :]) / SERIES
    turn = np.stack([np.cos(angle), np.sin(angle)]).astype(np.float32)
    last = []
    for parity in range(2):
        m = 2 * (x * 32 + zl * 4 + y) + parity
        angle = 2.0 * np.pi * (np.arange(128)[:, None] * m[None, :] % COLS) / COLS
        cos, sin = np.cos(angle), np.sin(angle)
        last.append(split(np.block([[cos, sin], [-sin, cos]])))
    return first, turn, np.stack(last)


def dot(left, right):
    return jnp.dot(left, right, preferred_element_type=jnp.float32)


def halves(value):
    high = value.astype(jnp.bfloat16)
    low = (value - high.astype(jnp.float32)).astype(jnp.bfloat16)
    return high, low


def kernel(
    cutoff_ref,
    wave_ref,
    mine_ref,
    other_ref,
    first_ref,
    turn_ref,
    last_ref,
    network_ref,
    loud_ref,
    masked,
    squares,
    piece,
    total,
):
    cutoff = cutoff_ref[0]
    slot = lax.broadcasted_iota(jnp.int32, (128, 128), 0)
    lane = lax.broadcasted_iota(jnp.int32, (128, 128), 1)
    base = ((slot // 32) * 64 + (slot % 8) * 8 + (slot // 8 % 4) * 2) * COLS + lane
    for parity in range(2):
        for block in range(2):
            keep = base + (parity * COLS + block * 128) < cutoff
            parts = []
            for comp in range(2):
                rows = [
                    wave_ref[:, pl.ds(y * 8 + parity * 4 + block * 2 + comp, 8, stride=32), :]
                    for y in range(4)
                ]
                value = jnp.stack(rows, axis=1).reshape(128, 128)
                parts.append(jnp.where(keep, value, 0.0))
            masked[parity, block, 0] = parts[0]
            masked[parity, block, 1] = parts[1]
            squares[parity, block] = parts[0] * parts[0] + parts[1] * parts[1]

    for half, data_ref in enumerate((mine_ref, other_ref)):
        for zh in range(2):
            energy = jnp.zeros((128, 128), jnp.float32)
            for parity in range(2):
                for block in range(2):
                    data = [
                        data_ref[
                            :, pl.ds(zh * 12 + comp * 4 + parity * 2 + block, 8, stride=24), :
                        ].reshape(128, 128)
                        for comp in range(3)
                    ]
                    wave_re = masked[parity, block, 0]
                    wave_im = masked[parity, block, 1]
                    energy = energy + squares[parity, block] * data[2]
                    lanes = slice(block * 128, block * 128 + 128)
                    high, low = halves(data[0] * wave_re + data[1] * wave_im)
                    piece[parity, 0, 0:128, lanes] = high
                    piece[parity, 1, 0:128, lanes] = low
                    high, low = halves(data[1] * wave_re - data[0] * wave_im)
                    piece[parity, 0, 128:256, lanes] = high
                    piece[parity, 1, 128:256, lanes] = low
            scale = 1.0 / jnp.sum(energy)
            start = half == 0 and zh == 0

            def chunk_step(chunk, carry):
                begin = pl.multiple_of(chunk * 256, 256)
                both = []
                for parity in range(2):
                    table = first_ref[parity, 0, pl.ds(begin, 256), :]
                    small = first_ref[parity, 1, pl.ds(begin, 256), :]
                    both.append(
                        dot(table, piece[parity, 0])
                        + dot(small, piece[parity, 0])
                        + dot(table, piece[parity, 1])
                    )
                for wrap in range(2):
                    section = both[0] - both[1] if wrap else both[0] + both[1]
                    section_re = section[0:128]
                    section_im = section[128:256]
                    place = pl.multiple_of(wrap * 256 + chunk * 128, 128)
                    cos = turn_ref[0, pl.ds(place, 128), :]
                    sin = turn_ref[1, pl.ds(place, 128), :]
                    twist_re = section_re * cos - section_im * sin
                    twist_im = section_re * sin + section_im * cos
                    for parity in range(2):
                        if parity:
                            fold_re = twist_re[:, :128] - twist_re[:, 128:]
                            fold_im = twist_im[:, :128] - twist_im[:, 128:]
                        else:
                            fold_re = twist_re[:, :128] + twist_re[:, 128:]
                            fold_im = twist_im[:, :128] + twist_im[:, 128:]
                        high, low = halves(jnp.concatenate([fold_re, fold_im], axis=1))
                        table = last_ref[parity, 0]
                        small = last_ref[parity, 1]
                        out = dot(high, table) + dot(high, small) + dot(low, table)
                        out_re = out[:, :128]
                        out_im = out[:, 128:]
                        power = (out_re * out_re + out_im * out_im) * scale
                        if not start:
                            power = power + total[parity, pl.ds(place, 128), :]
                        total[parity, pl.ds(place, 128), :] = power
                return carry

            lax.fori_loop(0, 2, chunk_step, 0)

    for parity in range(2):
        for block in range(4):
            value = total[parity, block * 128 : block * 128 + 128, :].T
            value = value.reshape(4, 4, 8, 128)
            for y in range(4):
                network_ref[:, pl.ds(y * 8 + parity * 4 + block, 8, stride=32), :] = value[:, y]
                loud_ref[:, y, parity, pl.ds(block, 8, stride=4), :] = value[:, y]


def shards(strain, inverse_noise, slides, templates, cutoffs):
    first, turn, last = tables()
    bank = (lax.axis_index("x") * 8 + lax.axis_index("zl")) * 4 + lax.axis_index("y")
    bins = (bank * 2 + jnp.arange(2, dtype=jnp.int32)[:, None]) * COLS + jnp.arange(
        COLS, dtype=jnp.int32
    )[None, :]
    angle = ((bins * slides[0]) & (SERIES - 1)).astype(jnp.float32) * (2.0 * np.pi / SERIES)
    cos, sin = jnp.cos(angle), jnp.sin(angle)
    noise = inverse_noise[0]
    data_re = strain[0, :, 0, :]
    data_im = strain[0, :, 1, :]
    shard = jnp.stack(
        [(data_re * cos - data_im * sin) * noise, (data_re * sin + data_im * cos) * noise, noise]
    ).reshape(3, 4, 128)
    pile = lax.all_to_all(jnp.broadcast_to(shard[None], (16, 3, 4, 128)), PILE, 0, 0)
    pile = pile.reshape(192, 128)
    mine = lax.all_to_all(jnp.broadcast_to(pile[None], (16, 192, 128)), PLANE, 0, 0)
    other = lax.ppermute(mine, "core", [(0, 1), (1, 0)])
    waves = templates.reshape(ROWS, 2, 2, 128).transpose(0, 2, 1, 3).reshape(4, 256, 128)
    vmem = pl.BlockSpec(memory_space=pltpu.VMEM)
    network, loud = pl.pallas_call(
        kernel,
        out_shape=(
            jax.ShapeDtypeStruct((4, 256, 128), jnp.float32),
            jax.ShapeDtypeStruct((4, 4, 2, 32, 128), jnp.float32),
        ),
        in_specs=[pl.BlockSpec(memory_space=pltpu.SMEM)] + [vmem] * 6,
        out_specs=(vmem, vmem),
        scratch_shapes=[
            pltpu.VMEM((2, 2, 2, 128, 128), jnp.float32),
            pltpu.VMEM((2, 2, 128, 128), jnp.float32),
            pltpu.VMEM((2, 2, 256, 256), jnp.bfloat16),
            pltpu.VMEM((2, 512, 128), jnp.float32),
        ],
        compiler_params=pltpu.CompilerParams(vmem_limit_bytes=32 * 1024 * 1024),
        cost_estimate=pl.CostEstimate(
            flops=3 * 2 * 537 * 10**6, bytes_accessed=8 * 2**20, transcendentals=0
        ),
    )(cutoffs, waves, mine, other, first, turn, last)
    swapped = lax.all_to_all(loud.reshape(32, 32, 128), CHIP, 0, 0)
    peak = jnp.max(swapped, axis=0).reshape(8, 1, 4, 128)
    peak = jnp.broadcast_to(peak, (8, 4, 4, 128)).reshape(32, 4, 128)
    peaks = lax.all_to_all(peak, STACK, 0, 0)
    loudest = jnp.max(peaks.reshape(16, 2, 4, 128), axis=0).reshape(1024)
    return (loudest, network.reshape(1, SERIES))


def solution(mesh):
    fine = Mesh(mesh.devices.reshape(4, 8, 4, 2, 2), ("x", "zl", "y", "zh", "core"))
    bank = ("x", "zl", "y")
    det = ("zh", "core")
    return jax.shard_map(
        shards,
        mesh=fine,
        in_specs=(
            P(det, bank, None, None),
            P(det, bank, None),
            P(det),
            P(bank + det, None, None, None),
            P(bank + det),
        ),
        out_specs=(P(bank), P(bank + det, None)),
        check_vma=False,
    )
```

```python
import jax
import jax.numpy as jnp
import ml_dtypes
import numpy as np
from jax import lax
from jax.experimental import pallas as pl
from jax.experimental.pallas import tpu as pltpu
from jax.sharding import Mesh, PartitionSpec as P

ROWS = 256
COLS = 256
SPAN = 512
SERIES = 131072
PLANE = ("x", "y")
PILE = ("zl", "zh")
CHIP = ("x", "y", "core")
STACK = ("zl", "zh", "core")


def split(values):
    high = values.astype(ml_dtypes.bfloat16)
    low = (values - high.astype(np.float64)).astype(ml_dtypes.bfloat16)
    return np.stack([high, low])


def plane_order():
    slot = np.arange(128)
    return slot // 32, slot // 8 % 4, slot % 8


def tables():
    x, y, zl = plane_order()
    first = []
    for parity in range(2):
        row = x * 64 + zl * 8 + y * 2 + parity
        angle = 2.0 * np.pi * (np.arange(256)[:, None] * row[None, :] % SPAN) / SPAN
        cos, sin = np.cos(angle), np.sin(angle)
        whole = []
        for chunk in range(2):
            part = slice(chunk * 128, chunk * 128 + 128)
            whole.append(np.block([[cos[part], -sin[part]], [sin[part], cos[part]]]))
        first.append(split(np.concatenate(whole)))
    first = np.stack(first)
    angle = 2.0 * np.pi * (np.arange(SPAN)[:, None] * np.arange(COLS)[None, :]) / SERIES
    turn = np.stack([np.cos(angle), np.sin(angle)]).astype(np.float32)
    last = []
    for parity in range(2):
        m = 2 * (x * 32 + zl * 4 + y) + parity
        angle = 2.0 * np.pi * (np.arange(128)[:, None] * m[None, :] % COLS) / COLS
        cos, sin = np.cos(angle), np.sin(angle)
        last.append(split(np.block([[cos, sin], [-sin, cos]])))
    return first, turn, np.stack(last)


def dot(left, right):
    return jnp.dot(left, right, preferred_element_type=jnp.float32)


def halves(value):
    high = value.astype(jnp.bfloat16)
    low = (value - high.astype(jnp.float32)).astype(jnp.bfloat16)
    return high, low


def prepare(slide_ref, strain_ref, noise_ref, out_ref):
    bank = (lax.axis_index("x") * 8 + lax.axis_index("zl")) * 4 + lax.axis_index("y")
    slot = lax.broadcasted_iota(jnp.int32, (4, 128), 0)
    lane = lax.broadcasted_iota(jnp.int32, (4, 128), 1)
    bins = bank * (2 * COLS) + slot * 128 + lane
    angle = ((bins * slide_ref[0]) & (SERIES - 1)).astype(jnp.float32) * (2.0 * np.pi / SERIES)
    cos, sin = jnp.cos(angle), jnp.sin(angle)
    data_re = strain_ref[pl.ds(0, 4, stride=2), :]
    data_im = strain_ref[pl.ds(1, 4, stride=2), :]
    noise = jnp.concatenate([noise_ref[i : i + 1, :] for i in (0, 2, 1, 3)])
    turned_re = (data_re * cos - data_im * sin) * noise
    turned_im = (data_re * sin + data_im * cos) * noise
    for peer in range(16):
        out_ref[peer, 0] = turned_re
        out_ref[peer, 1] = turned_im
        out_ref[peer, 2] = noise


def mask_waves(cutoff, wave_ref, masked):
    slot = lax.broadcasted_iota(jnp.int32, (128, 128), 0)
    lane = lax.broadcasted_iota(jnp.int32, (128, 128), 1)
    base = ((slot // 32) * 64 + (slot % 8) * 8 + (slot // 8 % 4) * 2) * COLS + lane
    for parity in range(2):
        for block in range(2):
            keep = base + (parity * COLS + block * 128) < cutoff
            for comp in range(2):
                rows = [
                    wave_ref[:, pl.ds(y * 8 + parity * 4 + block * 2 + comp, 8, stride=32), :]
                    for y in range(4)
                ]
                value = jnp.stack(rows, axis=1).reshape(128, 128)
                masked[parity, block, comp] = jnp.where(keep, value, 0.0)


def product(data_ref, zh, masked, piece):
    energy = jnp.zeros((128, 128), jnp.float32)
    for parity in range(2):
        for block in range(2):
            data = [
                data_ref[
                    :, pl.ds(zh * 12 + comp * 4 + parity * 2 + block, 8, stride=24), :
                ].reshape(128, 128)
                for comp in range(3)
            ]
            wave_re = masked[parity, block, 0]
            wave_im = masked[parity, block, 1]
            energy = energy + (wave_re * wave_re + wave_im * wave_im) * data[2]
            lanes = slice(block * 128, block * 128 + 128)
            high, low = halves(data[0] * wave_re + data[1] * wave_im)
            piece[zh, parity, 0, 0:128, lanes] = high
            piece[zh, parity, 1, 0:128, lanes] = low
            high, low = halves(data[1] * wave_re - data[0] * wave_im)
            piece[zh, parity, 0, 128:256, lanes] = high
            piece[zh, parity, 1, 128:256, lanes] = low
    return 1.0 / jnp.sum(energy)


def first_stage(zh, chunk, first_ref, piece):
    both = []
    for parity in range(2):
        table = first_ref[parity, 0, chunk * 256 : chunk * 256 + 256, :]
        small = first_ref[parity, 1, chunk * 256 : chunk * 256 + 256, :]
        both.append(
            dot(table, piece[zh, parity, 0])
            + dot(small, piece[zh, parity, 0])
            + dot(table, piece[zh, parity, 1])
        )
    return both


def last_stage(chunk, both, scale, turn_ref, last_ref, add):
    for wrap in range(2):
        section = both[0] - both[1] if wrap else both[0] + both[1]
        section_re = section[0:128]
        section_im = section[128:256]
        place = wrap * 256 + chunk * 128
        cos = turn_ref[0, place : place + 128, :]
        sin = turn_ref[1, place : place + 128, :]
        twist_re = section_re * cos - section_im * sin
        twist_im = section_re * sin + section_im * cos
        for parity in range(2):
            if parity:
                fold_re = twist_re[:, :128] - twist_re[:, 128:]
                fold_im = twist_im[:, :128] - twist_im[:, 128:]
            else:
                fold_re = twist_re[:, :128] + twist_re[:, 128:]
                fold_im = twist_im[:, :128] + twist_im[:, 128:]
            high, low = halves(jnp.concatenate([fold_re, fold_im], axis=1))
            table = last_ref[parity, 0]
            small = last_ref[parity, 1]
            out = dot(high, table) + dot(high, small) + dot(low, table)
            out_re = out[:, :128]
            out_im = out[:, 128:]
            add(parity, place, (out_re * out_re + out_im * out_im) * scale)


def pipeline(data_ref, masked, first_ref, turn_ref, last_ref, piece, add):
    steps = [(zh, chunk) for zh in range(2) for chunk in range(2)]
    scales = [product(data_ref, 0, masked, piece)]
    held = first_stage(0, 0, first_ref, piece)
    for step, (zh, chunk) in enumerate(steps):
        if step == 0:
            scales.append(product(data_ref, 1, masked, piece))
        after = first_stage(*steps[step + 1], first_ref, piece) if step < 3 else None
        last_stage(chunk, held, scales[zh], turn_ref, last_ref, add[zh])
        held = after


def own_kernel(cutoff_ref, wave_ref, data_ref, first_ref, turn_ref, last_ref, total, masked, piece):
    mask_waves(cutoff_ref[0], wave_ref, masked)

    def begin(parity, place, power):
        total[parity, place : place + 128, :] = power

    def more(parity, place, power):
        total[parity, place : place + 128, :] += power

    pipeline(data_ref, masked, first_ref, turn_ref, last_ref, piece, (begin, more))


def rest_kernel(
    masked, carry_ref, data_ref, first_ref, turn_ref, last_ref, network_ref, loud_ref, total, piece
):
    def more(parity, place, power):
        total[parity, place : place + 128, :] = carry_ref[parity, place : place + 128, :] + power

    def close(parity, place, power):
        block = place // 128
        value = (total[parity, place : place + 128, :] + power).T.reshape(4, 4, 8, 128)
        for y in range(4):
            network_ref[:, pl.ds(y * 8 + parity * 4 + block, 8, stride=32), :] = value[:, y]
            loud_ref[:, y, parity, pl.ds(block, 8, stride=4), :] = value[:, y]

    pipeline(data_ref, masked, first_ref, turn_ref, last_ref, piece, (more, close))


def shards(strain, inverse_noise, slides, templates, cutoffs):
    first, turn, last = tables()
    smem = pl.BlockSpec(memory_space=pltpu.SMEM)
    vmem = pl.BlockSpec(memory_space=pltpu.VMEM)
    params = pltpu.CompilerParams(vmem_limit_bytes=32 * 1024 * 1024)
    cost = pl.CostEstimate(flops=3 * 537 * 10**6, bytes_accessed=6 * 2**20, transcendentals=0)
    shard = pl.pallas_call(
        prepare,
        out_shape=jax.ShapeDtypeStruct((16, 3, 4, 128), jnp.float32),
        in_specs=[smem, vmem, vmem],
        out_specs=vmem,
    )(
        slides,
        strain.reshape(2, 2, 2, 128).transpose(0, 2, 1, 3).reshape(8, 128),
        inverse_noise.reshape(2, 2, 128).transpose(1, 0, 2).reshape(4, 128),
    )
    pile = lax.all_to_all(shard, PILE, 0, 0).reshape(192, 128)
    mine = lax.all_to_all(jnp.broadcast_to(pile[None], (16, 192, 128)), PLANE, 0, 0)
    other = lax.ppermute(mine, "core", [(0, 1), (1, 0)])
    waves = templates.reshape(ROWS, 2, 2, 128).transpose(0, 2, 1, 3).reshape(4, 256, 128)
    carry, masked = pl.pallas_call(
        own_kernel,
        out_shape=(
            jax.ShapeDtypeStruct((2, 512, 128), jnp.float32),
            jax.ShapeDtypeStruct((2, 2, 2, 128, 128), jnp.float32),
        ),
        in_specs=[smem] + [vmem] * 5,
        out_specs=(vmem, vmem),
        scratch_shapes=[pltpu.VMEM((2, 2, 2, 256, 256), jnp.bfloat16)],
        compiler_params=params,
        cost_estimate=cost,
    )(cutoffs, waves, mine, first, turn, last)
    network, loud = pl.pallas_call(
        rest_kernel,
        out_shape=(
            jax.ShapeDtypeStruct((4, 256, 128), jnp.float32),
            jax.ShapeDtypeStruct((4, 4, 2, 32, 128), jnp.float32),
        ),
        in_specs=[vmem] * 6,
        out_specs=(vmem, vmem),
        scratch_shapes=[
            pltpu.VMEM((2, 512, 128), jnp.float32),
            pltpu.VMEM((2, 2, 2, 256, 256), jnp.bfloat16),
        ],
        compiler_params=params,
        cost_estimate=cost,
    )(masked, carry, other, first, turn, last)
    swapped = lax.all_to_all(loud.reshape(32, 32, 128), CHIP, 0, 0)
    peak = jnp.max(swapped, axis=0).reshape(8, 1, 4, 128)
    peak = jnp.broadcast_to(peak, (8, 4, 4, 128)).reshape(32, 4, 128)
    peaks = lax.all_to_all(peak, STACK, 0, 0)
    loudest = jnp.max(peaks.reshape(16, 2, 4, 128), axis=0).reshape(1024)
    return (loudest, network.reshape(1, SERIES))


def solution(mesh):
    fine = Mesh(mesh.devices.reshape(4, 8, 4, 2, 2), ("x", "zl", "y", "zh", "core"))
    bank = ("x", "zl", "y")
    det = ("zh", "core")
    return jax.shard_map(
        shards,
        mesh=fine,
        in_specs=(
            P(det, bank, None, None),
            P(det, bank, None),
            P(det),
            P(bank + det, None, None, None),
            P(bank + det),
        ),
        out_specs=(P(bank), P(bank + det, None)),
        check_vma=False,
    )
```

```python
import jax
import jax.numpy as jnp
import ml_dtypes
import numpy as np
from jax import lax
from jax.experimental import pallas as pl
from jax.experimental.pallas import tpu as pltpu
from jax.sharding import Mesh, PartitionSpec as P

ROWS = 256
COLS = 256
SPAN = 512
SERIES = 131072
AXES = ("x1", "x0", "z2", "z1", "z0", "y1", "y0", "zh", "core")
BANK = AXES[:7]
DET = AXES[7:]
PLANE = ("x1", "y1", "x0", "y0")
PILE = ("zh", "z2", "z1", "z0")
CHIP = ("x1", "x0", "y1", "y0", "core")
STACK = ("z2", "z1", "z0", "zh", "core")


def split(values):
    high = values.astype(ml_dtypes.bfloat16)
    low = (values - high.astype(np.float64)).astype(ml_dtypes.bfloat16)
    return np.stack([high, low])


def slot_rows(slot):
    x = slot // 64 * 2 + slot // 16 % 2
    y = slot // 32 % 2 * 2 + slot // 8 % 2
    return x * 64 + slot % 8 * 8 + y * 2


def tables():
    slot = np.arange(128)
    first = []
    for parity in range(2):
        row = slot_rows(slot) + parity
        angle = 2.0 * np.pi * (np.arange(256)[:, None] * row[None, :] % SPAN) / SPAN
        cos, sin = np.cos(angle), np.sin(angle)
        whole = []
        for chunk in range(2):
            part = slice(chunk * 128, chunk * 128 + 128)
            whole.append(np.block([[cos[part], -sin[part]], [sin[part], cos[part]]]))
        first.append(split(np.concatenate(whole)))
    first = np.stack(first)
    angle = 2.0 * np.pi * (np.arange(SPAN)[:, None] * np.arange(COLS)[None, :]) / SERIES
    turn = np.stack([np.cos(angle), np.sin(angle)]).astype(np.float32)
    last = []
    for parity in range(2):
        m = 2 * (slot // 32 * 32 + slot % 8 * 4 + slot // 8 % 4) + parity
        angle = 2.0 * np.pi * (np.arange(128)[:, None] * m[None, :] % COLS) / COLS
        cos, sin = np.cos(angle), np.sin(angle)
        last.append(split(np.block([[cos, sin], [-sin, cos]])))
    return first, turn, np.stack(last)


def dot(left, right):
    return jnp.dot(left, right, preferred_element_type=jnp.float32)


def halves(value):
    high = value.astype(jnp.bfloat16)
    low = (value - high.astype(jnp.float32)).astype(jnp.bfloat16)
    return high, low


def prepare(
    slides_hbm, cutoffs_hbm, strain_hbm, noise_hbm, out_ref, cut_ref, slide, cutoff, strain, noise, sems
):
    pairs = ((slides_hbm, slide), (cutoffs_hbm, cutoff), (strain_hbm, strain), (noise_hbm, noise))
    copies = [pltpu.make_async_copy(a, b, sems.at[i]) for i, (a, b) in enumerate(pairs)]
    for copy in copies:
        copy.start()
    bank = jnp.int32(0)
    for name in BANK:
        bank = bank * 2 + lax.axis_index(name)
    slot = lax.broadcasted_iota(jnp.int32, (4, 128), 0)
    lane = lax.broadcasted_iota(jnp.int32, (4, 128), 1)
    bins = bank * (2 * COLS) + slot * 128 + lane
    for copy in copies:
        copy.wait()
    cut_ref[...] = jnp.full((8, 128), cutoff[0], jnp.int32)
    angle = ((bins * slide[0]) & (SERIES - 1)).astype(jnp.float32) * (2.0 * np.pi / SERIES)
    cos, sin = jnp.cos(angle), jnp.sin(angle)
    data_re = strain[pl.ds(0, 4, stride=2), :]
    data_im = strain[pl.ds(1, 4, stride=2), :]
    weight = jnp.concatenate([noise[i : i + 1, :] for i in (0, 2, 1, 3)])
    turned_re = (data_re * cos - data_im * sin) * weight
    turned_im = (data_re * sin + data_im * cos) * weight
    for peer in range(16):
        out_ref[peer, 0] = turned_re
        out_ref[peer, 1] = turned_im
        out_ref[peer, 2] = weight


def mask_waves(cut_ref, wave_ref, masked):
    cutoff = cut_ref[0:1, :]
    slot = lax.broadcasted_iota(jnp.int32, (128, 128), 0)
    lane = lax.broadcasted_iota(jnp.int32, (128, 128), 1)
    base = slot_rows(slot) * COLS + lane
    for parity in range(2):
        for block in range(2):
            keep = base + (parity * COLS + block * 128) < cutoff
            for comp in range(2):
                value = jnp.concatenate(
                    [
                        wave_ref[slot_rows(8 * i) * 4 // 256, pl.ds(
                            slot_rows(8 * i) * 4 % 256 + parity * 4 + block * 2 + comp, 8, stride=32
                        ), :]
                        for i in range(16)
                    ]
                )
                masked[parity, block, comp] = jnp.where(keep, value, 0.0)


def product(data_ref, zh, masked, piece):
    energy = jnp.zeros((128, 128), jnp.float32)
    for parity in range(2):
        for block in range(2):
            data = [
                data_ref[
                    :, pl.ds(zh * 96 + comp * 4 + parity * 2 + block, 8, stride=12), :
                ].reshape(128, 128)
                for comp in range(3)
            ]
            wave_re = masked[parity, block, 0]
            wave_im = masked[parity, block, 1]
            energy = energy + (wave_re * wave_re + wave_im * wave_im) * data[2]
            lanes = slice(block * 128, block * 128 + 128)
            high, low = halves(data[0] * wave_re + data[1] * wave_im)
            piece[zh, parity, 0, 0:128, lanes] = high
            piece[zh, parity, 1, 0:128, lanes] = low
            high, low = halves(data[1] * wave_re - data[0] * wave_im)
            piece[zh, parity, 0, 128:256, lanes] = high
            piece[zh, parity, 1, 128:256, lanes] = low
    return 1.0 / jnp.sum(energy)


def first_stage(zh, chunk, first_ref, piece):
    both = []
    for parity in range(2):
        table = first_ref[parity, 0, chunk * 256 : chunk * 256 + 256, :]
        small = first_ref[parity, 1, chunk * 256 : chunk * 256 + 256, :]
        both.append(
            dot(table, piece[zh, parity, 0])
            + dot(small, piece[zh, parity, 0])
            + dot(table, piece[zh, parity, 1])
        )
    return both


def last_stage(chunk, both, scale, turn_ref, last_ref, add):
    for wrap in range(2):
        section = both[0] - both[1] if wrap else both[0] + both[1]
        section_re = section[0:128]
        section_im = section[128:256]
        place = wrap * 256 + chunk * 128
        cos = turn_ref[0, place : place + 128, :]
        sin = turn_ref[1, place : place + 128, :]
        twist_re = section_re * cos - section_im * sin
        twist_im = section_re * sin + section_im * cos
        for parity in range(2):
            if parity:
                fold_re = twist_re[:, :128] - twist_re[:, 128:]
                fold_im = twist_im[:, :128] - twist_im[:, 128:]
            else:
                fold_re = twist_re[:, :128] + twist_re[:, 128:]
                fold_im = twist_im[:, :128] + twist_im[:, 128:]
            high, low = halves(jnp.concatenate([fold_re, fold_im], axis=1))
            table = last_ref[parity, 0]
            small = last_ref[parity, 1]
            out = dot(high, table) + dot(high, small) + dot(low, table)
            out_re = out[:, :128]
            out_im = out[:, 128:]
            add(parity, place, (out_re * out_re + out_im * out_im) * scale)


def pipeline(data_ref, masked, first_ref, turn_ref, last_ref, piece, add):
    steps = [(zh, chunk) for zh in range(2) for chunk in range(2)]
    scales = [product(data_ref, 0, masked, piece)]
    held = first_stage(0, 0, first_ref, piece)
    for step, (zh, chunk) in enumerate(steps):
        if step == 0:
            scales.append(product(data_ref, 1, masked, piece))
        after = first_stage(*steps[step + 1], first_ref, piece) if step < 3 else None
        last_stage(chunk, held, scales[zh], turn_ref, last_ref, add[zh])
        held = after


def own_kernel(cut_ref, wave_ref, data_ref, first_ref, turn_ref, last_ref, total, masked, piece):
    mask_waves(cut_ref, wave_ref, masked)

    def begin(parity, place, power):
        total[parity, place : place + 128, :] = power

    def more(parity, place, power):
        total[parity, place : place + 128, :] += power

    pipeline(data_ref, masked, first_ref, turn_ref, last_ref, piece, (begin, more))


def rest_kernel(
    masked, carry_ref, data_ref, first_ref, turn_ref, last_ref, network_ref, loud_ref, total, piece
):
    def more(parity, place, power):
        total[parity, place : place + 128, :] = carry_ref[parity, place : place + 128, :] + power

    def close(parity, place, power):
        block = place // 128
        value = (total[parity, place : place + 128, :] + power).T.reshape(4, 4, 8, 128)
        for y in range(4):
            network_ref[:, pl.ds(y * 8 + parity * 4 + block, 8, stride=32), :] = value[:, y]
            loud_ref[:, y, parity, pl.ds(block, 8, stride=4), :] = value[:, y]

    pipeline(data_ref, masked, first_ref, turn_ref, last_ref, piece, (more, close))


def shards(strain, inverse_noise, slides, templates, cutoffs):
    first, turn, last = tables()
    vmem = pl.BlockSpec(memory_space=pltpu.VMEM)
    params = pltpu.CompilerParams(vmem_limit_bytes=32 * 1024 * 1024)
    cost = pl.CostEstimate(flops=3 * 537 * 10**6, bytes_accessed=6 * 2**20, transcendentals=0)
    shard, cut = pl.pallas_call(
        prepare,
        out_shape=(
            jax.ShapeDtypeStruct((16, 3, 4, 128), jnp.float32),
            jax.ShapeDtypeStruct((8, 128), jnp.int32),
        ),
        in_specs=[pl.BlockSpec(memory_space=pltpu.HBM)] * 4,
        out_specs=(vmem, vmem),
        scratch_shapes=[
            pltpu.SMEM((1,), jnp.int32),
            pltpu.SMEM((1,), jnp.int32),
            pltpu.VMEM((8, 128), jnp.float32),
            pltpu.VMEM((4, 128), jnp.float32),
            pltpu.SemaphoreType.DMA((4,)),
        ],
    )(
        slides,
        cutoffs,
        strain.reshape(2, 2, 2, 128).transpose(0, 2, 1, 3).reshape(8, 128),
        inverse_noise.reshape(2, 2, 128).transpose(1, 0, 2).reshape(4, 128),
    )
    pile = lax.all_to_all(shard, PILE, 0, 0).reshape(192, 128)
    mine = lax.all_to_all(jnp.broadcast_to(pile[None], (16, 192, 128)), PLANE, 0, 0)
    other = lax.ppermute(mine, "core", [(0, 1), (1, 0)])
    waves = templates.reshape(ROWS, 2, 2, 128).transpose(0, 2, 1, 3).reshape(4, 256, 128)
    carry, masked = pl.pallas_call(
        own_kernel,
        out_shape=(
            jax.ShapeDtypeStruct((2, 512, 128), jnp.float32),
            jax.ShapeDtypeStruct((2, 2, 2, 128, 128), jnp.float32),
        ),
        in_specs=[vmem] * 6,
        out_specs=(vmem, vmem),
        scratch_shapes=[pltpu.VMEM((2, 2, 2, 256, 256), jnp.bfloat16)],
        compiler_params=params,
        cost_estimate=cost,
    )(cut, waves, mine, first, turn, last)
    network, loud = pl.pallas_call(
        rest_kernel,
        out_shape=(
            jax.ShapeDtypeStruct((4, 256, 128), jnp.float32),
            jax.ShapeDtypeStruct((4, 4, 2, 32, 128), jnp.float32),
        ),
        in_specs=[vmem] * 6,
        out_specs=(vmem, vmem),
        scratch_shapes=[
            pltpu.VMEM((2, 512, 128), jnp.float32),
            pltpu.VMEM((2, 2, 2, 256, 256), jnp.bfloat16),
        ],
        compiler_params=params,
        cost_estimate=cost,
    )(masked, carry, other, first, turn, last)
    swapped = lax.all_to_all(loud.reshape(32, 32, 128), CHIP, 0, 0)
    peak = jnp.max(swapped, axis=0).reshape(8, 1, 4, 128)
    peak = jnp.broadcast_to(peak, (8, 4, 4, 128)).reshape(32, 4, 128)
    peaks = lax.all_to_all(peak, STACK, 0, 0)
    loudest = jnp.max(peaks.reshape(16, 2, 4, 128), axis=0).reshape(1024)
    return (loudest, network.reshape(1, SERIES))


def solution(mesh):
    fine = Mesh(mesh.devices.reshape((2,) * 9), AXES)
    return jax.shard_map(
        shards,
        mesh=fine,
        in_specs=(
            P(DET, BANK, None, None),
            P(DET, BANK, None),
            P(DET),
            P(AXES, None, None, None),
            P(AXES),
        ),
        out_specs=(P(BANK), P(AXES, None)),
        check_vma=False,
    )
```

```python
import jax
import jax.numpy as jnp
import ml_dtypes
import numpy as np
from jax import lax
from jax.experimental import pallas as pl
from jax.experimental.pallas import tpu as pltpu
from jax.sharding import Mesh, PartitionSpec as P

ROWS = 256
COLS = 256
SPAN = 512
SERIES = 131072
AXES = ("x1", "x0", "z2", "z1", "z0", "y1", "y0", "zh", "core")
BANK = AXES[:7]
DET = AXES[7:]
PLANE = ("x1", "y1", "x0", "y0")
PILE = ("zh", "z2", "z1", "z0")
CHIP = ("x1", "x0", "y1", "y0", "core")
STACK = ("z2", "z1", "z0", "zh", "core")


def split(values):
    high = values.astype(ml_dtypes.bfloat16)
    low = (values - high.astype(np.float64)).astype(ml_dtypes.bfloat16)
    return np.stack([high, low])


def slot_rows(slot):
    x = slot // 64 * 2 + slot // 16 % 2
    y = slot // 32 % 2 * 2 + slot // 8 % 2
    return x * 64 + slot % 8 * 8 + y * 2


def tables():
    slot = np.arange(128)
    first = []
    for parity in range(2):
        row = slot_rows(slot) + parity
        angle = 2.0 * np.pi * (np.arange(256)[:, None] * row[None, :] % SPAN) / SPAN
        cos, sin = np.cos(angle), np.sin(angle)
        whole = []
        for chunk in range(2):
            part = slice(chunk * 128, chunk * 128 + 128)
            whole.append(np.block([[cos[part], -sin[part]], [sin[part], cos[part]]]))
        first.append(split(np.concatenate(whole)))
    first = np.stack(first)
    angle = 2.0 * np.pi * (np.arange(SPAN)[:, None] * np.arange(COLS)[None, :]) / SERIES
    turn = np.stack([np.cos(angle), np.sin(angle)]).astype(np.float32)
    last = []
    for parity in range(2):
        m = 2 * (slot // 32 * 32 + slot % 8 * 4 + slot // 8 % 4) + parity
        angle = 2.0 * np.pi * (np.arange(128)[:, None] * m[None, :] % COLS) / COLS
        cos, sin = np.cos(angle), np.sin(angle)
        last.append(split(np.block([[cos, sin], [-sin, cos]])))
    return first, turn, np.stack(last)


def dot(left, right):
    return jnp.dot(left, right, preferred_element_type=jnp.float32)


def halves(value):
    high = value.astype(jnp.bfloat16)
    low = (value - high.astype(jnp.float32)).astype(jnp.bfloat16)
    return high, low


def prepare(slide_ref, strain_ref, noise_ref, out_ref):
    bank = jnp.int32(0)
    for name in BANK:
        bank = bank * 2 + lax.axis_index(name)
    slot = lax.broadcasted_iota(jnp.int32, (4, 128), 0)
    lane = lax.broadcasted_iota(jnp.int32, (4, 128), 1)
    bins = bank * (2 * COLS) + slot * 128 + lane
    angle = ((bins * slide_ref[0]) & (SERIES - 1)).astype(jnp.float32) * (2.0 * np.pi / SERIES)
    cos, sin = jnp.cos(angle), jnp.sin(angle)
    data_re = strain_ref[pl.ds(0, 4, stride=2), :]
    data_im = strain_ref[pl.ds(1, 4, stride=2), :]
    weight = jnp.concatenate([noise_ref[i : i + 1, :] for i in (0, 2, 1, 3)])
    turned_re = (data_re * cos - data_im * sin) * weight
    turned_im = (data_re * sin + data_im * cos) * weight
    for peer in range(16):
        out_ref[peer, 0] = turned_re
        out_ref[peer, 1] = turned_im
        out_ref[peer, 2] = weight


def mask_waves(cut_ref, wave_ref, masked):
    cutoff = cut_ref[0:1, :]
    slot = lax.broadcasted_iota(jnp.int32, (128, 128), 0)
    lane = lax.broadcasted_iota(jnp.int32, (128, 128), 1)
    base = slot_rows(slot) * COLS + lane
    for parity in range(2):
        for block in range(2):
            keep = base + (parity * COLS + block * 128) < cutoff
            for comp in range(2):
                value = jnp.concatenate(
                    [
                        wave_ref[slot_rows(8 * i) * 4 // 256, pl.ds(
                            slot_rows(8 * i) * 4 % 256 + parity * 4 + block * 2 + comp, 8, stride=32
                        ), :]
                        for i in range(16)
                    ]
                )
                masked[parity, block, comp] = jnp.where(keep, value, 0.0)


def product(data_ref, zh, masked, piece):
    energy = jnp.zeros((128, 128), jnp.float32)
    for parity in range(2):
        for block in range(2):
            data = [
                data_ref[
                    :, pl.ds(zh * 96 + comp * 4 + parity * 2 + block, 8, stride=12), :
                ].reshape(128, 128)
                for comp in range(3)
            ]
            wave_re = masked[parity, block, 0]
            wave_im = masked[parity, block, 1]
            energy = energy + (wave_re * wave_re + wave_im * wave_im) * data[2]
            lanes = slice(block * 128, block * 128 + 128)
            high, low = halves(data[0] * wave_re + data[1] * wave_im)
            piece[zh, parity, 0, 0:128, lanes] = high
            piece[zh, parity, 1, 0:128, lanes] = low
            high, low = halves(data[1] * wave_re - data[0] * wave_im)
            piece[zh, parity, 0, 128:256, lanes] = high
            piece[zh, parity, 1, 128:256, lanes] = low
    return 1.0 / jnp.sum(energy)


def first_stage(zh, chunk, first_ref, piece):
    both = []
    for parity in range(2):
        table = first_ref[parity, 0, chunk * 256 : chunk * 256 + 256, :]
        small = first_ref[parity, 1, chunk * 256 : chunk * 256 + 256, :]
        both.append(
            dot(table, piece[zh, parity, 0])
            + dot(small, piece[zh, parity, 0])
            + dot(table, piece[zh, parity, 1])
        )
    return both


def last_stage(chunk, both, scale, turn_ref, last_ref, add):
    for wrap in range(2):
        section = both[0] - both[1] if wrap else both[0] + both[1]
        section_re = section[0:128]
        section_im = section[128:256]
        place = wrap * 256 + chunk * 128
        cos = turn_ref[0, place : place + 128, :]
        sin = turn_ref[1, place : place + 128, :]
        twist_re = section_re * cos - section_im * sin
        twist_im = section_re * sin + section_im * cos
        for parity in range(2):
            if parity:
                fold_re = twist_re[:, :128] - twist_re[:, 128:]
                fold_im = twist_im[:, :128] - twist_im[:, 128:]
            else:
                fold_re = twist_re[:, :128] + twist_re[:, 128:]
                fold_im = twist_im[:, :128] + twist_im[:, 128:]
            high, low = halves(jnp.concatenate([fold_re, fold_im], axis=1))
            table = last_ref[parity, 0]
            small = last_ref[parity, 1]
            out = dot(high, table) + dot(high, small) + dot(low, table)
            out_re = out[:, :128]
            out_im = out[:, 128:]
            add(parity, place, (out_re * out_re + out_im * out_im) * scale)


def pipeline(data_ref, masked, first_ref, turn_ref, last_ref, piece, add):
    steps = [(zh, chunk) for zh in range(2) for chunk in range(2)]
    scales = [product(data_ref, 0, masked, piece)]
    held = first_stage(0, 0, first_ref, piece)
    for step, (zh, chunk) in enumerate(steps):
        if step == 0:
            scales.append(product(data_ref, 1, masked, piece))
        after = first_stage(*steps[step + 1], first_ref, piece) if step < 3 else None
        last_stage(chunk, held, scales[zh], turn_ref, last_ref, add[zh])
        held = after


def own_kernel(cut_ref, wave_ref, data_ref, first_ref, turn_ref, last_ref, total, masked, piece):
    mask_waves(cut_ref, wave_ref, masked)

    def begin(parity, place, power):
        total[parity, place : place + 128, :] = power

    def more(parity, place, power):
        total[parity, place : place + 128, :] += power

    pipeline(data_ref, masked, first_ref, turn_ref, last_ref, piece, (begin, more))


def rest_kernel(
    masked, carry_ref, data_ref, first_ref, turn_ref, last_ref, network_ref, loud_ref, total, piece
):
    def more(parity, place, power):
        total[parity, place : place + 128, :] = carry_ref[parity, place : place + 128, :] + power

    def close(parity, place, power):
        block = place // 128
        value = (total[parity, place : place + 128, :] + power).T.reshape(4, 4, 8, 128)
        for y in range(4):
            network_ref[:, pl.ds(y * 8 + parity * 4 + block, 8, stride=32), :] = value[:, y]
            loud_ref[:, y, parity, pl.ds(block, 8, stride=4), :] = value[:, y]

    pipeline(data_ref, masked, first_ref, turn_ref, last_ref, piece, (more, close))


def shards(strain, inverse_noise, slides, templates, cutoffs):
    first, turn, last = tables()
    vmem = pl.BlockSpec(memory_space=pltpu.VMEM)
    params = pltpu.CompilerParams(vmem_limit_bytes=32 * 1024 * 1024)
    cost = pl.CostEstimate(flops=3 * 537 * 10**6, bytes_accessed=6 * 2**20, transcendentals=0)
    cut = jnp.broadcast_to(cutoffs[:, None], (8, 128))
    shard = pl.pallas_call(
        prepare,
        out_shape=pltpu.VMEM((16, 3, 4, 128), jnp.float32),
        in_specs=[pl.BlockSpec(memory_space=pltpu.SMEM), vmem, vmem],
        out_specs=vmem,
    )(
        slides,
        strain.reshape(2, 2, 2, 128).transpose(0, 2, 1, 3).reshape(8, 128),
        inverse_noise.reshape(2, 2, 128).transpose(1, 0, 2).reshape(4, 128),
    )
    pile = lax.all_to_all(shard, PILE, 0, 0).reshape(192, 128)
    mine = lax.all_to_all(jnp.broadcast_to(pile[None], (16, 192, 128)), PLANE, 0, 0)
    other = lax.ppermute(mine, "core", [(0, 1), (1, 0)])
    waves = templates.reshape(ROWS, 2, 2, 128).transpose(0, 2, 1, 3).reshape(4, 256, 128)
    carry, masked = pl.pallas_call(
        own_kernel,
        out_shape=(
            jax.ShapeDtypeStruct((2, 512, 128), jnp.float32),
            jax.ShapeDtypeStruct((2, 2, 2, 128, 128), jnp.float32),
        ),
        in_specs=[vmem] * 6,
        out_specs=(vmem, vmem),
        scratch_shapes=[pltpu.VMEM((2, 2, 2, 256, 256), jnp.bfloat16)],
        compiler_params=params,
        cost_estimate=cost,
    )(cut, waves, mine, first, turn, last)
    network, loud = pl.pallas_call(
        rest_kernel,
        out_shape=(
            pltpu.VMEM((4, 256, 128), jnp.float32),
            jax.ShapeDtypeStruct((4, 4, 2, 32, 128), jnp.float32),
        ),
        in_specs=[vmem] * 6,
        out_specs=(vmem, vmem),
        scratch_shapes=[
            pltpu.VMEM((2, 512, 128), jnp.float32),
            pltpu.VMEM((2, 2, 2, 256, 256), jnp.bfloat16),
        ],
        compiler_params=params,
        cost_estimate=cost,
    )(masked, carry, other, first, turn, last)
    swapped = lax.all_to_all(loud.reshape(32, 32, 128), CHIP, 0, 0)
    peak = jnp.max(swapped, axis=0).reshape(8, 1, 4, 128)
    peak = jnp.broadcast_to(peak, (8, 4, 4, 128)).reshape(32, 4, 128)
    peaks = lax.all_to_all(peak, STACK, 0, 0)
    loudest = jnp.max(peaks.reshape(16, 2, 4, 128), axis=0).reshape(1024)
    return (loudest, network.reshape(1, SERIES))


def solution(mesh):
    fine = Mesh(mesh.devices.reshape((2,) * 9), AXES)
    return jax.shard_map(
        shards,
        mesh=fine,
        in_specs=(
            P(DET, BANK, None, None),
            P(DET, BANK, None),
            P(DET),
            P(AXES, None, None, None),
            P(AXES),
        ),
        out_specs=(P(BANK), P(AXES, None)),
        check_vma=False,
    )
```

```python
import jax
import jax.numpy as jnp
import ml_dtypes
import numpy as np
from jax import lax
from jax.experimental import pallas as pl
from jax.experimental.pallas import tpu as pltpu
from jax.sharding import Mesh, PartitionSpec as P

ROWS = 256
COLS = 256
SPAN = 512
SERIES = 131072
AXES = ("x1", "x0", "z2", "z1", "z0", "y1", "y0", "zh", "core")
BANK = AXES[:7]
DET = AXES[7:]
PLANE = ("x1", "y1", "x0", "y0")
PILE = ("zh", "z2", "z1", "z0")
CHIP = ("x1", "x0", "y1", "y0", "core")
STACK = ("z2", "z1", "z0", "zh", "core")


def split(values):
    high = values.astype(ml_dtypes.bfloat16)
    low = (values - high.astype(np.float64)).astype(ml_dtypes.bfloat16)
    return np.stack([high, low])


def slot_rows(slot):
    x = 3 - slot // 64 * 2 - slot // 16 % 2
    y = 3 - slot // 32 % 2 * 2 - slot // 8 % 2
    return x * 64 + slot % 8 * 8 + y * 2


def tables():
    slot = np.arange(128)
    first = []
    for parity in range(2):
        row = slot_rows(slot) + parity
        angle = 2.0 * np.pi * (np.arange(256)[:, None] * row[None, :] % SPAN) / SPAN
        cos, sin = np.cos(angle), np.sin(angle)
        whole = []
        for chunk in range(2):
            part = slice(chunk * 128, chunk * 128 + 128)
            whole.append(np.block([[cos[part], -sin[part]], [sin[part], cos[part]]]))
        first.append(split(np.concatenate(whole)))
    first = np.stack(first)
    angle = 2.0 * np.pi * (np.arange(SPAN)[:, None] * np.arange(COLS)[None, :]) / SERIES
    turn = np.stack([np.cos(angle), np.sin(angle)]).astype(np.float32)
    last = []
    for parity in range(2):
        m = 2 * (slot // 32 * 32 + slot % 8 * 4 + slot // 8 % 4) + parity
        angle = 2.0 * np.pi * (np.arange(128)[:, None] * m[None, :] % COLS) / COLS
        cos, sin = np.cos(angle), np.sin(angle)
        last.append(split(np.block([[cos, sin], [-sin, cos]])))
    return first, turn, np.stack(last)


def dot(left, right):
    return jnp.dot(left, right, preferred_element_type=jnp.float32)


def halves(value):
    high = value.astype(jnp.bfloat16)
    low = (value - high.astype(jnp.float32)).astype(jnp.bfloat16)
    return high, low


def prepare(slide_ref, strain_ref, noise_ref, out_ref):
    bank = jnp.int32(0)
    for name in BANK:
        bank = bank * 2 + lax.axis_index(name)
    slot = lax.broadcasted_iota(jnp.int32, (4, 128), 0)
    lane = lax.broadcasted_iota(jnp.int32, (4, 128), 1)
    bins = bank * (2 * COLS) + slot * 128 + lane
    angle = ((bins * slide_ref[0]) & (SERIES - 1)).astype(jnp.float32) * (2.0 * np.pi / SERIES)
    cos, sin = jnp.cos(angle), jnp.sin(angle)
    data_re = strain_ref[pl.ds(0, 4, stride=2), :]
    data_im = strain_ref[pl.ds(1, 4, stride=2), :]
    weight = jnp.concatenate([noise_ref[i : i + 1, :] for i in (0, 2, 1, 3)])
    turned_re = (data_re * cos - data_im * sin) * weight
    turned_im = (data_re * sin + data_im * cos) * weight
    for peer in range(16):
        out_ref[peer, 0] = turned_re
        out_ref[peer, 1] = turned_im
        out_ref[peer, 2] = weight


def mask_waves(cut_ref, wave_ref, masked):
    cutoff = cut_ref[0:1, :]
    slot = lax.broadcasted_iota(jnp.int32, (128, 128), 0)
    lane = lax.broadcasted_iota(jnp.int32, (128, 128), 1)
    base = slot_rows(slot) * COLS + lane
    for parity in range(2):
        for block in range(2):
            keep = base + (parity * COLS + block * 128) < cutoff
            for comp in range(2):
                value = jnp.concatenate(
                    [
                        wave_ref[slot_rows(8 * i) * 4 // 256, pl.ds(
                            slot_rows(8 * i) * 4 % 256 + parity * 4 + block * 2 + comp, 8, stride=32
                        ), :]
                        for i in range(16)
                    ]
                )
                masked[parity, block, comp] = jnp.where(keep, value, 0.0)


def product(data_ref, zh, masked, piece):
    energy = jnp.zeros((128, 128), jnp.float32)
    for parity in range(2):
        for block in range(2):
            data = [
                data_ref[
                    :, pl.ds(zh * 96 + comp * 4 + parity * 2 + block, 8, stride=12), :
                ].reshape(128, 128)
                for comp in range(3)
            ]
            wave_re = masked[parity, block, 0]
            wave_im = masked[parity, block, 1]
            energy = energy + (wave_re * wave_re + wave_im * wave_im) * data[2]
            lanes = slice(block * 128, block * 128 + 128)
            high, low = halves(data[0] * wave_re + data[1] * wave_im)
            piece[zh, parity, 0, 0:128, lanes] = high
            piece[zh, parity, 1, 0:128, lanes] = low
            high, low = halves(data[1] * wave_re - data[0] * wave_im)
            piece[zh, parity, 0, 128:256, lanes] = high
            piece[zh, parity, 1, 128:256, lanes] = low
    return 1.0 / jnp.sum(energy)


def first_stage(zh, chunk, first_ref, piece):
    both = []
    for parity in range(2):
        table = first_ref[parity, 0, chunk * 256 : chunk * 256 + 256, :]
        small = first_ref[parity, 1, chunk * 256 : chunk * 256 + 256, :]
        both.append(
            dot(table, piece[zh, parity, 0])
            + dot(small, piece[zh, parity, 0])
            + dot(table, piece[zh, parity, 1])
        )
    return both


def last_stage(chunk, both, scale, turn_ref, last_ref, add):
    for wrap in range(2):
        section = both[0] - both[1] if wrap else both[0] + both[1]
        section_re = section[0:128]
        section_im = section[128:256]
        place = wrap * 256 + chunk * 128
        cos = turn_ref[0, place : place + 128, :]
        sin = turn_ref[1, place : place + 128, :]
        twist_re = section_re * cos - section_im * sin
        twist_im = section_re * sin + section_im * cos
        for parity in range(2):
            if parity:
                fold_re = twist_re[:, :128] - twist_re[:, 128:]
                fold_im = twist_im[:, :128] - twist_im[:, 128:]
            else:
                fold_re = twist_re[:, :128] + twist_re[:, 128:]
                fold_im = twist_im[:, :128] + twist_im[:, 128:]
            high, low = halves(jnp.concatenate([fold_re, fold_im], axis=1))
            table = last_ref[parity, 0]
            small = last_ref[parity, 1]
            out = dot(high, table) + dot(high, small) + dot(low, table)
            out_re = out[:, :128]
            out_im = out[:, 128:]
            add(parity, place, (out_re * out_re + out_im * out_im) * scale)


def pipeline(data_ref, masked, first_ref, turn_ref, last_ref, piece, add):
    steps = [(zh, chunk) for zh in range(2) for chunk in range(2)]
    scales = [product(data_ref, 0, masked, piece)]
    held = first_stage(0, 0, first_ref, piece)
    for step, (zh, chunk) in enumerate(steps):
        if step == 0:
            scales.append(product(data_ref, 1, masked, piece))
        after = first_stage(*steps[step + 1], first_ref, piece) if step < 3 else None
        last_stage(chunk, held, scales[zh], turn_ref, last_ref, add[zh])
        held = after


def own_kernel(cut_ref, wave_ref, data_ref, first_ref, turn_ref, last_ref, total, masked, piece):
    mask_waves(cut_ref, wave_ref, masked)

    def begin(parity, place, power):
        total[parity, place : place + 128, :] = power

    def more(parity, place, power):
        total[parity, place : place + 128, :] += power

    pipeline(data_ref, masked, first_ref, turn_ref, last_ref, piece, (begin, more))


def rest_kernel(
    masked, carry_ref, data_ref, first_ref, turn_ref, last_ref, network_ref, loud_ref, total, piece
):
    def more(parity, place, power):
        total[parity, place : place + 128, :] = carry_ref[parity, place : place + 128, :] + power

    def close(parity, place, power):
        block = place // 128
        value = (total[parity, place : place + 128, :] + power).T.reshape(4, 4, 8, 128)
        for y in range(4):
            network_ref[:, pl.ds(y * 8 + parity * 4 + block, 8, stride=32), :] = value[:, y]
            for x in range(4):
                loud_ref[3 - x, 3 - y, parity, pl.ds(block, 8, stride=4), :] = value[x, y]

    pipeline(data_ref, masked, first_ref, turn_ref, last_ref, piece, (more, close))


def shards(strain, inverse_noise, slides, templates, cutoffs):
    first, turn, last = tables()
    vmem = pl.BlockSpec(memory_space=pltpu.VMEM)
    params = pltpu.CompilerParams(vmem_limit_bytes=32 * 1024 * 1024)
    cost = pl.CostEstimate(flops=3 * 537 * 10**6, bytes_accessed=6 * 2**20, transcendentals=0)
    cut = jnp.broadcast_to(cutoffs[:, None], (8, 128))
    shard = pl.pallas_call(
        prepare,
        out_shape=pltpu.VMEM((16, 3, 4, 128), jnp.float32),
        in_specs=[pl.BlockSpec(memory_space=pltpu.SMEM), vmem, vmem],
        out_specs=vmem,
    )(
        slides,
        strain.reshape(2, 2, 2, 128).transpose(0, 2, 1, 3).reshape(8, 128),
        inverse_noise.reshape(2, 2, 128).transpose(1, 0, 2).reshape(4, 128),
    )
    pile = lax.all_to_all(
        shard, PILE, 0, 0, axis_index_groups=[list(range(8, 16)) + list(range(8))]
    ).reshape(192, 128)
    mine = lax.all_to_all(jnp.broadcast_to(pile[None], (16, 192, 128)), PLANE, 0, 0, axis_index_groups=[list(range(15, -1, -1))])
    other = lax.ppermute(mine, "core", [(0, 1), (1, 0)])
    waves = templates.reshape(ROWS, 2, 2, 128).transpose(0, 2, 1, 3).reshape(4, 256, 128)
    carry, masked = pl.pallas_call(
        own_kernel,
        out_shape=(
            jax.ShapeDtypeStruct((2, 512, 128), jnp.float32),
            jax.ShapeDtypeStruct((2, 2, 2, 128, 128), jnp.float32),
        ),
        in_specs=[vmem] * 6,
        out_specs=(vmem, vmem),
        scratch_shapes=[pltpu.VMEM((2, 2, 2, 256, 256), jnp.bfloat16)],
        compiler_params=params,
        cost_estimate=cost,
    )(cut, waves, mine, first, turn, last)
    network, loud = pl.pallas_call(
        rest_kernel,
        out_shape=(
            pltpu.VMEM((4, 256, 128), jnp.float32),
            jax.ShapeDtypeStruct((4, 4, 2, 32, 128), jnp.float32),
        ),
        in_specs=[vmem] * 6,
        out_specs=(vmem, vmem),
        scratch_shapes=[
            pltpu.VMEM((2, 512, 128), jnp.float32),
            pltpu.VMEM((2, 2, 2, 256, 256), jnp.bfloat16),
        ],
        compiler_params=params,
        cost_estimate=cost,
    )(masked, carry, other, first, turn, last)
    swapped = lax.all_to_all(loud.reshape(32, 32, 128), CHIP, 0, 0, axis_index_groups=[list(range(31, -1, -1))])
    peak = jnp.max(swapped, axis=0).reshape(8, 1, 4, 128)[::-1]
    peak = jnp.broadcast_to(peak, (8, 4, 4, 128)).reshape(32, 4, 128)
    peaks = lax.all_to_all(peak, STACK, 0, 0, axis_index_groups=[list(range(31, -1, -1))])
    loudest = jnp.max(peaks.reshape(16, 2, 4, 128), axis=0).reshape(1024)
    return (loudest, network.reshape(1, SERIES))


def solution(mesh):
    fine = Mesh(mesh.devices.reshape((2,) * 9), AXES)
    return jax.shard_map(
        shards,
        mesh=fine,
        in_specs=(
            P(DET, BANK, None, None),
            P(DET, BANK, None),
            P(DET),
            P(AXES, None, None, None),
            P(AXES),
        ),
        out_specs=(P(BANK), P(AXES, None)),
        check_vma=False,
    )
```

```python
import jax
import jax.numpy as jnp
import ml_dtypes
import numpy as np
from jax import lax
from jax.experimental import pallas as pl
from jax.experimental.pallas import tpu as pltpu
from jax.sharding import Mesh, PartitionSpec as P

ROWS = 256
COLS = 256
SPAN = 512
SERIES = 131072
AXES = ("x1", "x0", "z2", "z1", "z0", "y1", "y0", "zh", "core")
BANK = AXES[:7]
DET = AXES[7:]
PLANE = ("x1", "y1", "x0", "y0")
PILE = ("zh", "z2", "z1", "z0")
CHIP = ("x1", "x0", "y1", "y0", "core")
STACK = ("z2", "z1", "z0", "zh", "core")


def split(values):
    high = values.astype(ml_dtypes.bfloat16)
    low = (values - high.astype(np.float64)).astype(ml_dtypes.bfloat16)
    return np.stack([high, low])


def slot_rows(slot):
    x = 3 - slot // 64 * 2 - slot // 16 % 2
    y = 3 - slot // 32 % 2 * 2 - slot // 8 % 2
    return x * 64 + slot % 8 * 8 + y * 2


def tables():
    slot = np.arange(128)
    first = []
    for parity in range(2):
        row = slot_rows(slot) + parity
        angle = 2.0 * np.pi * (np.arange(256)[:, None] * row[None, :] % SPAN) / SPAN
        cos, sin = np.cos(angle), np.sin(angle)
        whole = []
        for chunk in range(2):
            part = slice(chunk * 128, chunk * 128 + 128)
            whole.append(np.block([[cos[part], -sin[part]], [sin[part], cos[part]]]))
        first.append(split(np.concatenate(whole)))
    first = np.stack(first)
    angle = 2.0 * np.pi * (np.arange(SPAN)[:, None] * np.arange(COLS)[None, :]) / SERIES
    turn = np.stack([np.cos(angle), np.sin(angle)]).astype(np.float32)
    last = []
    for parity in range(2):
        m = 2 * (slot // 32 * 32 + slot % 8 * 4 + slot // 8 % 4) + parity
        angle = 2.0 * np.pi * (np.arange(128)[:, None] * m[None, :] % COLS) / COLS
        cos, sin = np.cos(angle), np.sin(angle)
        last.append(split(np.block([[cos, sin], [-sin, cos]])))
    return first, turn, np.stack(last)


def dot(left, right):
    return jnp.dot(left, right, preferred_element_type=jnp.float32)


def halves(value):
    high = value.astype(jnp.bfloat16)
    low = (value - high.astype(jnp.float32)).astype(jnp.bfloat16)
    return high, low


def prepare(slide_ref, strain_ref, noise_ref, out_ref):
    bank = jnp.int32(0)
    for name in BANK:
        bank = bank * 2 + lax.axis_index(name)
    slot = lax.broadcasted_iota(jnp.int32, (4, 128), 0)
    lane = lax.broadcasted_iota(jnp.int32, (4, 128), 1)
    bins = bank * (2 * COLS) + slot * 128 + lane
    angle = ((bins * slide_ref[0]) & (SERIES - 1)).astype(jnp.float32) * (2.0 * np.pi / SERIES)
    cos, sin = jnp.cos(angle), jnp.sin(angle)
    data_re = strain_ref[pl.ds(0, 4, stride=2), :]
    data_im = strain_ref[pl.ds(1, 4, stride=2), :]
    weight = jnp.concatenate([noise_ref[i : i + 1, :] for i in (0, 2, 1, 3)])
    turned_re = (data_re * cos - data_im * sin) * weight
    turned_im = (data_re * sin + data_im * cos) * weight
    for peer in range(16):
        out_ref[peer, 0] = turned_re
        out_ref[peer, 1] = turned_im
        out_ref[peer, 2] = weight


def mask_waves(cut_ref, wave_ref, masked):
    cutoff = cut_ref[0:1, :]
    slot = lax.broadcasted_iota(jnp.int32, (128, 128), 0)
    lane = lax.broadcasted_iota(jnp.int32, (128, 128), 1)
    base = slot_rows(slot) * COLS + lane
    for parity in range(2):
        for block in range(2):
            keep = base + (parity * COLS + block * 128) < cutoff
            for comp in range(2):
                value = jnp.concatenate(
                    [
                        wave_ref[slot_rows(8 * i) * 4 // 256, pl.ds(
                            slot_rows(8 * i) * 4 % 256 + parity * 4 + block * 2 + comp, 8, stride=32
                        ), :]
                        for i in range(16)
                    ]
                )
                masked[parity, block, comp] = jnp.where(keep, value, 0.0)


def product(data_ref, zh, masked, piece):
    energy = jnp.zeros((128, 128), jnp.float32)
    for parity in range(2):
        for block in range(2):
            data = [
                data_ref[
                    :, pl.ds(zh * 96 + comp * 4 + parity * 2 + block, 8, stride=12), :
                ].reshape(128, 128)
                for comp in range(3)
            ]
            wave_re = masked[parity, block, 0]
            wave_im = masked[parity, block, 1]
            energy = energy + (wave_re * wave_re + wave_im * wave_im) * data[2]
            lanes = slice(block * 128, block * 128 + 128)
            high, low = halves(data[0] * wave_re + data[1] * wave_im)
            piece[zh, parity, 0, 0:128, lanes] = high
            piece[zh, parity, 1, 0:128, lanes] = low
            high, low = halves(data[1] * wave_re - data[0] * wave_im)
            piece[zh, parity, 0, 128:256, lanes] = high
            piece[zh, parity, 1, 128:256, lanes] = low
    return 1.0 / jnp.sum(energy)


def first_stage(zh, chunk, first_ref, piece):
    both = []
    for parity in range(2):
        table = first_ref[parity, 0, chunk * 256 : chunk * 256 + 256, :]
        small = first_ref[parity, 1, chunk * 256 : chunk * 256 + 256, :]
        both.append(
            dot(table, piece[zh, parity, 0])
            + dot(small, piece[zh, parity, 0])
            + dot(table, piece[zh, parity, 1])
        )
    return both


def last_stage(chunk, both, scale, turn_ref, last_ref, add):
    for wrap in range(2):
        section = both[0] - both[1] if wrap else both[0] + both[1]
        section_re = section[0:128]
        section_im = section[128:256]
        place = wrap * 256 + chunk * 128
        cos = turn_ref[0, place : place + 128, :]
        sin = turn_ref[1, place : place + 128, :]
        twist_re = section_re * cos - section_im * sin
        twist_im = section_re * sin + section_im * cos
        for parity in range(2):
            if parity:
                fold_re = twist_re[:, :128] - twist_re[:, 128:]
                fold_im = twist_im[:, :128] - twist_im[:, 128:]
            else:
                fold_re = twist_re[:, :128] + twist_re[:, 128:]
                fold_im = twist_im[:, :128] + twist_im[:, 128:]
            high, low = halves(jnp.concatenate([fold_re, fold_im], axis=1))
            table = last_ref[parity, 0]
            small = last_ref[parity, 1]
            out = dot(high, table) + dot(high, small) + dot(low, table)
            out_re = out[:, :128]
            out_im = out[:, 128:]
            add(parity, place, (out_re * out_re + out_im * out_im) * scale)


def pipeline(data_ref, masked, first_ref, turn_ref, last_ref, piece, add):
    steps = [(zh, chunk) for zh in range(2) for chunk in range(2)]
    scales = [product(data_ref, 0, masked, piece)]
    held = first_stage(0, 0, first_ref, piece)
    for step, (zh, chunk) in enumerate(steps):
        if step == 0:
            scales.append(product(data_ref, 1, masked, piece))
        after = first_stage(*steps[step + 1], first_ref, piece) if step < 3 else None
        last_stage(chunk, held, scales[zh], turn_ref, last_ref, add[zh])
        held = after


def own_kernel(cut_ref, wave_ref, data_ref, first_ref, turn_ref, last_ref, total, masked, piece):
    mask_waves(cut_ref, wave_ref, masked)

    def begin(parity, place, power):
        total[parity, place : place + 128, :] = power

    def more(parity, place, power):
        total[parity, place : place + 128, :] += power

    pipeline(data_ref, masked, first_ref, turn_ref, last_ref, piece, (begin, more))


def rest_kernel(
    masked, carry_ref, data_ref, first_ref, turn_ref, last_ref, network_ref, loud_ref, total, piece
):
    def more(parity, place, power):
        total[parity, place : place + 128, :] = carry_ref[parity, place : place + 128, :] + power

    def close(parity, place, power):
        block = place // 128
        value = (total[parity, place : place + 128, :] + power).T.reshape(4, 4, 8, 128)
        for y in range(4):
            network_ref[:, pl.ds(y * 8 + parity * 4 + block, 8, stride=32), :] = value[:, y]
            for x in range(4):
                loud_ref[3 - x, 3 - y, 1 - parity, pl.ds(block, 8, stride=4), :] = value[x, y]

    pipeline(data_ref, masked, first_ref, turn_ref, last_ref, piece, (more, close))


def shards(strain, inverse_noise, slides, templates, cutoffs):
    first, turn, last = tables()
    vmem = pl.BlockSpec(memory_space=pltpu.VMEM)
    params = pltpu.CompilerParams(vmem_limit_bytes=32 * 1024 * 1024)
    cost = pl.CostEstimate(flops=3 * 537 * 10**6, bytes_accessed=6 * 2**20, transcendentals=0)
    cut = jnp.broadcast_to(cutoffs[:, None], (8, 128))
    shard = pl.pallas_call(
        prepare,
        out_shape=pltpu.VMEM((16, 3, 4, 128), jnp.float32),
        in_specs=[pl.BlockSpec(memory_space=pltpu.SMEM), vmem, vmem],
        out_specs=vmem,
    )(
        slides,
        strain.reshape(2, 2, 2, 128).transpose(0, 2, 1, 3).reshape(8, 128),
        inverse_noise.reshape(2, 2, 128).transpose(1, 0, 2).reshape(4, 128),
    )
    pile = lax.all_to_all(
        shard, PILE, 0, 0, axis_index_groups=[list(range(8, 16)) + list(range(8))]
    ).reshape(192, 128)
    mine = lax.all_to_all(jnp.broadcast_to(pile[None], (16, 192, 128)), PLANE, 0, 0, axis_index_groups=[list(range(15, -1, -1))])
    other = lax.ppermute(mine, "core", [(0, 1), (1, 0)])
    waves = templates.reshape(ROWS, 2, 2, 128).transpose(0, 2, 1, 3).reshape(4, 256, 128)
    carry, masked = pl.pallas_call(
        own_kernel,
        out_shape=(
            jax.ShapeDtypeStruct((2, 512, 128), jnp.float32),
            jax.ShapeDtypeStruct((2, 2, 2, 128, 128), jnp.float32),
        ),
        in_specs=[vmem] * 6,
        out_specs=(vmem, vmem),
        scratch_shapes=[pltpu.VMEM((2, 2, 2, 256, 256), jnp.bfloat16)],
        compiler_params=params,
        cost_estimate=cost,
    )(cut, waves, mine, first, turn, last)
    network, loud = pl.pallas_call(
        rest_kernel,
        out_shape=(
            pltpu.VMEM((4, 256, 128), jnp.float32),
            jax.ShapeDtypeStruct((4, 4, 2, 32, 128), jnp.float32),
        ),
        in_specs=[vmem] * 6,
        out_specs=(vmem, vmem),
        scratch_shapes=[
            pltpu.VMEM((2, 512, 128), jnp.float32),
            pltpu.VMEM((2, 2, 2, 256, 256), jnp.bfloat16),
        ],
        compiler_params=params,
        cost_estimate=cost,
    )(masked, carry, other, first, turn, last)
    swapped = lax.all_to_all(loud.reshape(32, 32, 128), CHIP, 0, 0, axis_index_groups=[list(range(31, -1, -1))])
    peak = jnp.max(swapped, axis=0).reshape(8, 1, 4, 128)
    peak = jnp.broadcast_to(peak, (2, 8, 2, 4, 128)).reshape(32, 4, 128)
    peaks = lax.all_to_all(peak, STACK, 0, 0, axis_index_groups=[[z * 4 + h * 2 + c for h in (1, 0) for z in range(8) for c in (0, 1)]])
    loudest = jnp.max(peaks.reshape(16, 2, 4, 128), axis=0).reshape(1024)
    return (loudest, network.reshape(1, SERIES))


def solution(mesh):
    fine = Mesh(mesh.devices.reshape((2,) * 9), AXES)
    return jax.shard_map(
        shards,
        mesh=fine,
        in_specs=(
            P(DET, BANK, None, None),
            P(DET, BANK, None),
            P(DET),
            P(AXES, None, None, None),
            P(AXES),
        ),
        out_specs=(P(BANK), P(AXES, None)),
        check_vma=False,
    )
```

```python
import jax
import jax.numpy as jnp
import ml_dtypes
import numpy as np
from jax import lax
from jax.experimental import pallas as pl
from jax.experimental.pallas import tpu as pltpu
from jax.sharding import Mesh, PartitionSpec as P

ROWS = 256
COLS = 256
SPAN = 512
SERIES = 131072
AXES = ("x1", "x0", "z2", "z1", "z0", "y1", "y0", "zh", "core")
BANK = AXES[:7]
DET = AXES[7:]
PLANE = ("x1", "y1", "x0", "y0")
PILE = ("zh", "z2", "z1", "z0")
CHIP = ("x1", "x0", "y1", "y0", "core")
STACK = ("z2", "z1", "z0", "zh", "core")


def split(values):
    high = values.astype(ml_dtypes.bfloat16)
    low = (values - high.astype(np.float64)).astype(ml_dtypes.bfloat16)
    return np.stack([high, low])


def slot_rows(slot):
    x = 2 - slot // 64 * 2 + slot // 16 % 2
    y = 2 - slot // 32 % 2 * 2 + slot // 8 % 2
    return x * 64 + slot % 8 * 8 + y * 2


def tables():
    slot = np.arange(128)
    first = []
    for parity in range(2):
        row = slot_rows(slot) + parity
        angle = 2.0 * np.pi * (np.arange(256)[:, None] * row[None, :] % SPAN) / SPAN
        cos, sin = np.cos(angle), np.sin(angle)
        whole = []
        for chunk in range(2):
            part = slice(chunk * 128, chunk * 128 + 128)
            whole.append(np.block([[cos[part], -sin[part]], [sin[part], cos[part]]]))
        first.append(split(np.concatenate(whole)))
    first = np.stack(first)
    angle = 2.0 * np.pi * (np.arange(SPAN)[:, None] * np.arange(COLS)[None, :]) / SERIES
    turn = np.stack([np.cos(angle), np.sin(angle)]).astype(np.float32)
    last = []
    for parity in range(2):
        m = 2 * (slot // 32 * 32 + slot % 8 * 4 + slot // 8 % 4) + parity
        angle = 2.0 * np.pi * (np.arange(128)[:, None] * m[None, :] % COLS) / COLS
        cos, sin = np.cos(angle), np.sin(angle)
        last.append(split(np.block([[cos, sin], [-sin, cos]])))
    return first, turn, np.stack(last)


def dot(left, right):
    return jnp.dot(left, right, preferred_element_type=jnp.float32)


def halves(value):
    high = value.astype(jnp.bfloat16)
    low = (value - high.astype(jnp.float32)).astype(jnp.bfloat16)
    return high, low


def prepare(slide_ref, strain_ref, noise_ref, out_ref):
    bank = jnp.int32(0)
    for name in BANK:
        bank = bank * 2 + lax.axis_index(name)
    slot = lax.broadcasted_iota(jnp.int32, (4, 128), 0)
    lane = lax.broadcasted_iota(jnp.int32, (4, 128), 1)
    bins = bank * (2 * COLS) + slot * 128 + lane
    angle = ((bins * slide_ref[0]) & (SERIES - 1)).astype(jnp.float32) * (2.0 * np.pi / SERIES)
    cos, sin = jnp.cos(angle), jnp.sin(angle)
    data_re = strain_ref[pl.ds(0, 4, stride=2), :]
    data_im = strain_ref[pl.ds(1, 4, stride=2), :]
    weight = jnp.concatenate([noise_ref[i : i + 1, :] for i in (0, 2, 1, 3)])
    turned_re = (data_re * cos - data_im * sin) * weight
    turned_im = (data_re * sin + data_im * cos) * weight
    for peer in range(16):
        out_ref[peer, 0] = turned_re
        out_ref[peer, 1] = turned_im
        out_ref[peer, 2] = weight


def mask_waves(cut_ref, wave_ref, masked):
    cutoff = cut_ref[0:1, :]
    slot = lax.broadcasted_iota(jnp.int32, (128, 128), 0)
    lane = lax.broadcasted_iota(jnp.int32, (128, 128), 1)
    base = slot_rows(slot) * COLS + lane
    for parity in range(2):
        for block in range(2):
            keep = base + (parity * COLS + block * 128) < cutoff
            for comp in range(2):
                value = jnp.concatenate(
                    [
                        wave_ref[slot_rows(8 * i) * 4 // 256, pl.ds(
                            slot_rows(8 * i) * 4 % 256 + parity * 4 + block * 2 + comp, 8, stride=32
                        ), :]
                        for i in range(16)
                    ]
                )
                masked[parity, block, comp] = jnp.where(keep, value, 0.0)


def product(data_ref, zh, masked, piece):
    energy = jnp.zeros((128, 128), jnp.float32)
    for parity in range(2):
        for block in range(2):
            data = [
                data_ref[
                    :, pl.ds(zh * 96 + comp * 4 + parity * 2 + block, 8, stride=12), :
                ].reshape(128, 128)
                for comp in range(3)
            ]
            wave_re = masked[parity, block, 0]
            wave_im = masked[parity, block, 1]
            energy = energy + (wave_re * wave_re + wave_im * wave_im) * data[2]
            lanes = slice(block * 128, block * 128 + 128)
            high, low = halves(data[0] * wave_re + data[1] * wave_im)
            piece[zh, parity, 0, 0:128, lanes] = high
            piece[zh, parity, 1, 0:128, lanes] = low
            high, low = halves(data[1] * wave_re - data[0] * wave_im)
            piece[zh, parity, 0, 128:256, lanes] = high
            piece[zh, parity, 1, 128:256, lanes] = low
    return 1.0 / jnp.sum(energy)


def first_stage(zh, chunk, first_ref, piece):
    both = []
    for parity in range(2):
        table = first_ref[parity, 0, chunk * 256 : chunk * 256 + 256, :]
        small = first_ref[parity, 1, chunk * 256 : chunk * 256 + 256, :]
        both.append(
            dot(table, piece[zh, parity, 0])
            + dot(small, piece[zh, parity, 0])
            + dot(table, piece[zh, parity, 1])
        )
    return both


def last_stage(chunk, both, scale, turn_ref, last_ref, add):
    for wrap in range(2):
        section = both[0] - both[1] if wrap else both[0] + both[1]
        section_re = section[0:128]
        section_im = section[128:256]
        place = wrap * 256 + chunk * 128
        cos = turn_ref[0, place : place + 128, :]
        sin = turn_ref[1, place : place + 128, :]
        twist_re = section_re * cos - section_im * sin
        twist_im = section_re * sin + section_im * cos
        for parity in range(2):
            if parity:
                fold_re = twist_re[:, :128] - twist_re[:, 128:]
                fold_im = twist_im[:, :128] - twist_im[:, 128:]
            else:
                fold_re = twist_re[:, :128] + twist_re[:, 128:]
                fold_im = twist_im[:, :128] + twist_im[:, 128:]
            high, low = halves(jnp.concatenate([fold_re, fold_im], axis=1))
            table = last_ref[parity, 0]
            small = last_ref[parity, 1]
            out = dot(high, table) + dot(high, small) + dot(low, table)
            out_re = out[:, :128]
            out_im = out[:, 128:]
            add(parity, place, (out_re * out_re + out_im * out_im) * scale)


def pipeline(data_ref, masked, first_ref, turn_ref, last_ref, piece, add):
    steps = [(zh, chunk) for zh in range(2) for chunk in range(2)]
    scales = [product(data_ref, 0, masked, piece)]
    held = first_stage(0, 0, first_ref, piece)
    for step, (zh, chunk) in enumerate(steps):
        if step == 0:
            scales.append(product(data_ref, 1, masked, piece))
        after = first_stage(*steps[step + 1], first_ref, piece) if step < 3 else None
        last_stage(chunk, held, scales[zh], turn_ref, last_ref, add[zh])
        held = after


def own_kernel(cut_ref, wave_ref, data_ref, first_ref, turn_ref, last_ref, total, masked, piece):
    mask_waves(cut_ref, wave_ref, masked)

    def begin(parity, place, power):
        total[parity, place : place + 128, :] = power

    def more(parity, place, power):
        total[parity, place : place + 128, :] += power

    pipeline(data_ref, masked, first_ref, turn_ref, last_ref, piece, (begin, more))


def rest_kernel(
    masked, carry_ref, data_ref, first_ref, turn_ref, last_ref, network_ref, loud_ref, total, piece
):
    def more(parity, place, power):
        total[parity, place : place + 128, :] = carry_ref[parity, place : place + 128, :] + power

    def close(parity, place, power):
        block = place // 128
        value = (total[parity, place : place + 128, :] + power).T.reshape(4, 4, 8, 128)
        for y in range(4):
            network_ref[:, pl.ds(y * 8 + parity * 4 + block, 8, stride=32), :] = value[:, y]
            for x in range(4):
                loud_ref[x ^ 2, y ^ 2, parity, pl.ds(block, 8, stride=4), :] = value[x, y]

    pipeline(data_ref, masked, first_ref, turn_ref, last_ref, piece, (more, close))


def shards(strain, inverse_noise, slides, templates, cutoffs):
    first, turn, last = tables()
    vmem = pl.BlockSpec(memory_space=pltpu.VMEM)
    params = pltpu.CompilerParams(vmem_limit_bytes=32 * 1024 * 1024)
    cost = pl.CostEstimate(flops=3 * 537 * 10**6, bytes_accessed=6 * 2**20, transcendentals=0)
    cut = jnp.broadcast_to(cutoffs[:, None], (8, 128))
    shard = pl.pallas_call(
        prepare,
        out_shape=pltpu.VMEM((16, 3, 4, 128), jnp.float32),
        in_specs=[pl.BlockSpec(memory_space=pltpu.SMEM), vmem, vmem],
        out_specs=vmem,
    )(
        slides,
        strain.reshape(2, 2, 2, 128).transpose(0, 2, 1, 3).reshape(8, 128),
        inverse_noise.reshape(2, 2, 128).transpose(1, 0, 2).reshape(4, 128),
    )
    pile = lax.all_to_all(
        shard, PILE, 0, 0, axis_index_groups=[list(range(8, 16)) + list(range(8))]
    ).reshape(192, 128)
    mine = lax.all_to_all(jnp.broadcast_to(pile[None], (16, 192, 128)), PLANE, 0, 0, axis_index_groups=[[i ^ 12 for i in range(16)]])
    other = lax.ppermute(mine, "core", [(0, 1), (1, 0)])
    waves = templates.reshape(ROWS, 2, 2, 128).transpose(0, 2, 1, 3).reshape(4, 256, 128)
    carry, masked = pl.pallas_call(
        own_kernel,
        out_shape=(
            jax.ShapeDtypeStruct((2, 512, 128), jnp.float32),
            jax.ShapeDtypeStruct((2, 2, 2, 128, 128), jnp.float32),
        ),
        in_specs=[vmem] * 6,
        out_specs=(vmem, vmem),
        scratch_shapes=[pltpu.VMEM((2, 2, 2, 256, 256), jnp.bfloat16)],
        compiler_params=params,
        cost_estimate=cost,
    )(cut, waves, mine, first, turn, last)
    network, loud = pl.pallas_call(
        rest_kernel,
        out_shape=(
            pltpu.VMEM((4, 256, 128), jnp.float32),
            jax.ShapeDtypeStruct((4, 4, 2, 32, 128), jnp.float32),
        ),
        in_specs=[vmem] * 6,
        out_specs=(vmem, vmem),
        scratch_shapes=[
            pltpu.VMEM((2, 512, 128), jnp.float32),
            pltpu.VMEM((2, 2, 2, 256, 256), jnp.bfloat16),
        ],
        compiler_params=params,
        cost_estimate=cost,
    )(masked, carry, other, first, turn, last)
    swapped = lax.all_to_all(loud.reshape(32, 32, 128), CHIP, 0, 0, axis_index_groups=[[i ^ 20 for i in range(32)]])
    peak = jnp.max(swapped, axis=0).reshape(8, 1, 4, 128)
    peak = jnp.broadcast_to(peak, (2, 8, 2, 4, 128)).reshape(32, 4, 128)
    peaks = lax.all_to_all(peak, STACK, 0, 0, axis_index_groups=[[z * 4 + h * 2 + c for h in (1, 0) for z in range(8) for c in (0, 1)]])
    loudest = jnp.max(peaks.reshape(16, 2, 4, 128), axis=0).reshape(1024)
    return (loudest, network.reshape(1, SERIES))


def solution(mesh):
    fine = Mesh(mesh.devices.reshape((2,) * 9), AXES)
    return jax.shard_map(
        shards,
        mesh=fine,
        in_specs=(
            P(DET, BANK, None, None),
            P(DET, BANK, None),
            P(DET),
            P(AXES, None, None, None),
            P(AXES),
        ),
        out_specs=(P(BANK), P(AXES, None)),
        check_vma=False,
    )
```
